32 devices in a mesh: win: 4 (over z), rcv: 8 (over y, x, core).
Axes of the slice: x: 2, y: 2, z: 4, core: 2. Of those that a mesh axis runs over, the one named last changes fastest.
Arguments:
- spectra: bfloat16 [512, 16, 2, 1024], P('rcv', 'win'), may hold values from -6 to 6
- source_block: int32 [1], replicated, may hold values from 0 to 7
Outputs:
- correlations: bfloat16 [512, 64, 2048], P('rcv', None, 'win')
The draws below stay inside these ranges and needn't reach their ends.
All inputs are finite; a program needn't handle non-finite values.
Results may differ from the reference program's by a relative error of at most 0.015.
Values may be sent and summed in bfloat16 or wider, within the bound.
A program may use at most 256 MiB of HBM per device.

```python
import jax
import jax.numpy as jnp
from jax import lax

FREQS = 1024
LAGS = 2048
WINDOWS = 16
CH_DEV = 64
SOURCES = 64
CHANNELS = 512
N_RCV = 8


def block_levels(rng, shape, split, least, top_value):
    level = 1.0
    for position, shards_of in split:
        draws = jax.random.uniform(jax.random.fold_in(jax.random.fold_in(rng, 6), position), (shards_of,), jnp.float32, least / len(split), top_value / len(split))
        level = level * jnp.repeat(jnp.exp(draws), shape[position] // shards_of).reshape((-1,) + (1,) * (len(shape) - 1 - position))
    return level


def centred(own_key, shape, width, limit, cuts=(), held_as=jnp.bfloat16):
    entries = jax.random.normal(own_key, shape, jnp.float32) * width
    if len(cuts) > 0:
        entries = block_levels(own_key, shape, cuts, -0.22, 0.18) * entries
    return jnp.clip(entries, min=-limit, max=limit).astype(held_as)


def setup_inputs(seed: int = 0) -> dict:
    key_of = jax.random.split(jax.random.key(seed), 3)
    return {
        "spectra": centred(key_of[0], (CHANNELS, WINDOWS, 2, FREQS), 1.0, 6.0, ((0, 8), (1, 4))),
        "source_block": jax.random.randint(key_of[1], (1,), 0, N_RCV).astype(jnp.int32),
    }


def cross_block(receivers, source):
    flipped = jnp.stack([-receivers[:, :, 1], receivers[:, :, 0]], axis=2)
    real_part = jnp.einsum('rwcf,swcf->rsf', receivers, source)
    imag_part = jnp.einsum('rwcf,swcf->rsf', flipped, source)
    return (real_part, imag_part)

def reference(spectra, source_block):
    first_row = (source_block[0] * CH_DEV).astype(jnp.int32)
    source = lax.dynamic_slice_in_dim(spectra, first_row, SOURCES, 0).astype(jnp.float32)
    blocks = spectra.reshape(N_RCV, CH_DEV, WINDOWS, 2, FREQS)
    lag_scale = 1.0 / jnp.sqrt(jnp.float32(LAGS * WINDOWS))

    def per_block(receivers):
        real_part, imag_part = cross_block(receivers.astype(jnp.float32), source)
        real_part = lax.optimization_barrier(real_part.astype(jnp.bfloat16)).astype(jnp.float32)
        imag_part = lax.optimization_barrier(imag_part.astype(jnp.bfloat16)).astype(jnp.float32)
        spectrum = real_part + 1j * imag_part
        padded = jnp.concatenate([spectrum, jnp.zeros_like(spectrum)], axis=-1)
        series = jnp.fft.ifft(padded, axis=-1) * LAGS
        shifted = jnp.fft.fftshift(series, axes=-1)
        return (jnp.real(shifted) * lag_scale).astype(jnp.bfloat16)
    stacked = lax.map(per_block, blocks)
    return stacked.reshape(CHANNELS, SOURCES, LAGS)
```

```python
import functools
import math

import jax
import jax.numpy as jnp
import ml_dtypes
import numpy as np
from jax import lax
from jax.experimental import pallas as pl
from jax.experimental.pallas import tpu as pltpu
from jax.sharding import PartitionSpec as P

MESH = pl.DeviceIdType.MESH
LANES = 128
CHUNKS = 4


def lag_table(n_freqs, n_win, groups):
    n_lags = 2 * n_freqs
    column = np.arange(n_freqs)
    freq = (column % groups) * LANES + column // groups
    lag = (np.arange(n_lags) - n_freqs).reshape(n_win, 1, n_lags // n_win, 1)
    angle = (2.0 * math.pi / n_lags) * ((freq * lag) % n_lags)
    table = np.concatenate([np.cos(angle), -np.sin(angle)], axis=1)
    return table.astype(ml_dtypes.bfloat16)


def gather_kernel(n_win, n_rcv, root_ref, own_ref, recv_out, src_out, slots, piece_sem, sp_send, sp_recv,
                  r_send, r_recv, z_send, z_recv, x_send, x_recv, c_send, c_recv, local_sem):
    me_w = lax.axis_index("win")
    me_r = lax.axis_index("rcv")
    n_chan, rows = own_ref.shape[0], own_ref.shape[1]
    part = n_chan // n_rcv
    chunk = n_chan // CHUNKS
    sibling = me_r + 1 - 2 * lax.rem(me_r, 2)
    n_chip = n_rcv // 2

    barrier = pltpu.get_barrier_semaphore()

    @pl.when(me_w > 0)
    def _():
        pl.semaphore_signal(barrier, inc=1, device_id=(me_w - 1, me_r), device_id_type=MESH)

    @pl.when(me_w < n_win - 1)
    def _():
        pl.semaphore_signal(barrier, inc=1, device_id=(me_w + 1, me_r), device_id_type=MESH)

    @pl.loop(1, n_rcv)
    def _(d):
        pl.semaphore_signal(barrier, inc=1, device_id=(me_w, lax.rem(me_r + d, n_rcv)), device_id_type=MESH)

    on_line = (me_w > 0).astype(jnp.int32) + (me_w < n_win - 1).astype(jnp.int32)
    pl.semaphore_wait(barrier, n_rcv - 1 + on_line)

    def piece_copy(d):
        target = lax.rem(me_r + d, n_rcv)
        return pltpu.make_async_remote_copy(
            src_ref=own_ref.at[pl.ds(target * part, part)], dst_ref=slots.at[me_r],
            send_sem=sp_send.at[d], recv_sem=sp_recv.at[d],
            device_id=(me_w, target), device_id_type=MESH)

    def hop(buffer, first, count, origin, send_sem, recv_sem, step):
        block = buffer.at[pl.ds(first, count), pl.ds(origin * rows, rows), :]
        return pltpu.make_async_remote_copy(
            src_ref=block, dst_ref=block, send_sem=send_sem, recv_sem=recv_sem,
            device_id=(me_w + step, me_r), device_id_type=MESH)

    def recv_hop(c, t, way):
        step = 1 - 2 * way
        return hop(recv_out, c * chunk, chunk, me_w - step * t, r_send.at[way, t, c], r_recv.at[way, t, c], step)

    def src_hop(t, way):
        step = 1 - 2 * way
        return hop(src_out, me_r * part, part, me_w - step * t, z_send.at[way, t], z_recv.at[way, t], step)

    def can_send(t, way):
        return (me_w >= t) & (me_w < n_win - 1) if way == 0 else (me_w + t < n_win) & (me_w > 0)

    def can_receive(t, way):
        return me_w > t if way == 0 else me_w + t + 1 < n_win


    def recv_arrival(c, t, way):
        step = 1 - 2 * way
        return hop(recv_out, c * chunk, chunk, me_w - step * (t + 1), r_send.at[way, t, c], r_recv.at[way, t, c], 0)

    def src_arrival(t, way):
        step = 1 - 2 * way
        return hop(src_out, me_r * part, part, me_w - step * (t + 1), z_send.at[way, t], z_recv.at[way, t], 0)

    @pl.loop(1, n_rcv)
    def _(d):
        piece_copy(d).start()

    own_local = pltpu.make_async_copy(own_ref, recv_out.at[:, pl.ds(me_w * rows, rows), :], local_sem.at[0])
    own_local.start()
    piece_local = pltpu.make_async_copy(own_ref.at[pl.ds(me_r * part, part)], slots.at[me_r], local_sem.at[1])
    piece_local.start()
    own_local.wait()

    def start_own(c):
        for way in range(2):
            @pl.when(can_send(0, way))
            def _():
                recv_hop(c, 0, way).start()

    for c in range(CHUNKS):
        start_own(c)

    piece_local.wait()

    @pl.loop(1, n_rcv)
    def _(d):
        piece_copy(d).wait()

    piece_sem[...] = slots[root_ref[0]]
    mine = src_out.at[pl.ds(me_r * part, part), pl.ds(me_w * rows, rows), :]
    placed = pltpu.make_async_copy(piece_sem, mine, local_sem.at[2])
    placed.start()
    placed.wait()
    for way in range(2):
        @pl.when(can_send(0, way))
        def _():
            src_hop(0, way).start()
    for t in range(n_win - 1):
        for way in range(2):
            @pl.when(can_receive(t, way))
            def _():
                src_arrival(t, way).wait_recv()

            @pl.when(can_send(t + 1, way))
            def _():
                src_hop(t + 1, way).start()

    def block_copy(owner, target, send_sem, recv_sem):
        block = src_out.at[pl.ds(owner * part, part)]
        return pltpu.make_async_remote_copy(
            src_ref=block, dst_ref=block, send_sem=send_sem, recv_sem=recv_sem,
            device_id=(me_w, target), device_id_type=MESH)

    def chip_copy(d):
        return block_copy(me_r, lax.rem(me_r + 2 * d, n_rcv), x_send.at[d], x_recv.at[d])

    def core_copy(d):
        return block_copy(lax.rem(me_r - 2 * d + n_rcv, n_rcv), sibling, c_send.at[d], c_recv.at[d])

    def core_arrival(d):
        return block_copy(lax.rem(sibling - 2 * d + n_rcv, n_rcv), sibling, c_send.at[d], c_recv.at[d])

    def chip_arrival(d):
        return block_copy(lax.rem(me_r - 2 * d + n_rcv, n_rcv), sibling, x_send.at[d], x_recv.at[d])

    @pl.loop(1, n_chip)
    def _(d):
        chip_copy(d).start()

    core_copy(0).start()

    for c in range(CHUNKS):
        for t in range(n_win - 1):
            for way in range(2):
                @pl.when(can_receive(t, way))
                def _():
                    recv_arrival(c, t, way).wait_recv()

                @pl.when(can_send(t + 1, way))
                def _():
                    recv_hop(c, t + 1, way).start()

    @pl.loop(1, n_chip)
    def _(d):
        chip_arrival(d).wait_recv()
        core_copy(d).start()

    @pl.loop(0, n_chip)
    def _(d):
        core_arrival(d).wait_recv()
        core_copy(d).wait_send()

    @pl.loop(1, n_chip)
    def _(d):
        chip_copy(d).wait_send()

    for t in range(n_win - 1):
        for way in range(2):
            @pl.when(can_send(t, way))
            def _():
                src_hop(t, way).wait_send()
                for c in range(CHUNKS):
                    recv_hop(c, t, way).wait_send()


def gather(root, own, n_win, n_rcv):
    n_chan, rows, lanes = own.shape
    part = n_chan // n_rcv
    whole = jax.ShapeDtypeStruct((n_chan, n_win * rows, lanes), own.dtype)
    sem = pltpu.SemaphoreType.DMA
    return pl.pallas_call(
        functools.partial(gather_kernel, n_win, n_rcv),
        out_shape=(whole, whole),
        in_specs=[pl.BlockSpec(memory_space=pltpu.SMEM), pl.BlockSpec(memory_space=pl.ANY)],
        out_specs=(pl.BlockSpec(memory_space=pl.ANY), pl.BlockSpec(memory_space=pl.ANY)),
        scratch_shapes=[
            pltpu.VMEM((n_rcv, part, rows, lanes), own.dtype),
            pltpu.VMEM((part, rows, lanes), own.dtype),
            sem((n_rcv,)), sem((n_rcv,)),
            sem((2, n_win, CHUNKS)), sem((2, n_win, CHUNKS)),
            sem((2, n_win)), sem((2, n_win)),
            sem((n_rcv,)), sem((n_rcv,)),
            sem((n_rcv,)), sem((n_rcv,)),
            sem((3,)),
        ],
        compiler_params=pltpu.CompilerParams(
            collective_id=0, has_side_effects=True, vmem_limit_bytes=16 << 20),
        name="gather",
    )(root, own)


def store_turned(flipped, row, block):
    turned = block.astype(jnp.float32).T
    at = pl.ds(pl.multiple_of(row * LANES, LANES), LANES)
    for slab in range(flipped.shape[0]):
        flipped[slab, at, :] = turned[:, slab * LANES:(slab + 1) * LANES]


def load_turned(flipped, j, count):
    slabs = [flipped[slab, pl.ds(j, count, stride=LANES), :] for slab in range(flipped.shape[0])]
    return jnp.concatenate(slabs, axis=1)


def correlate_kernel(lag_scale, groups, r_ref, s_ref, table_ref, out_ref, flipped, weights, x_real, x_imag):
    n_src, depth, lanes = s_ref.shape
    n_chan = r_ref.shape[0]
    n_lags = table_ref.shape[1]
    lane = lax.broadcasted_iota(jnp.int32, (1, depth), 1)

    @pl.when(pl.program_id(0) == 0)
    def _():
        @pl.loop(0, n_src)
        def _(s):
            store_turned(flipped, s, s_ref[s])

        is_real = lax.rem(lane, 2 * groups) < groups

        @pl.loop(0, lanes)
        def _(j):
            spec = load_turned(flipped, j, n_src)
            turned = jnp.where(is_real, pltpu.roll(spec, depth - groups, 1), -pltpu.roll(spec, groups, 1))
            weights[j, :n_src, :] = spec.astype(jnp.bfloat16)
            weights[j, n_src:, :] = turned.astype(jnp.bfloat16)

    @pl.loop(0, n_chan)
    def _(r):
        store_turned(flipped, r, r_ref[r])

    row = lax.broadcasted_iota(jnp.int32, (groups, depth), 0)
    picked = (lax.rem(lax.broadcasted_iota(jnp.int32, (groups, depth), 1), groups) == row)[None]
    first_half = lax.broadcasted_iota(jnp.int32, (1, 1, 2 * n_src), 2) < n_src

    @pl.loop(0, lanes // 2)
    def _(jp):
        reals, imags = [], []
        for k in range(2):
            j = 2 * jp + k
            spec = load_turned(flipped, j, n_chan)
            spread = jnp.where(picked, spec[:, None, :], 0.0).reshape(n_chan * groups, depth).astype(jnp.bfloat16)
            real = weights[j, :n_src, :]
            imag = weights[j, n_src:, :]
            both = jnp.concatenate([real, real, imag, imag], axis=0)
            cross = lax.dot_general(spread, both, (((1,), (1,)), ((), ())), preferred_element_type=jnp.float32)
            for half, kept in ((0, reals), (1, imags)):
                part = cross[:, half * 2 * n_src:(half + 1) * 2 * n_src].reshape(n_chan // 2, 2, groups, 2 * n_src)
                kept.append(jnp.where(first_half, part[:, 0], part[:, 1]))
        at = pl.ds(pl.multiple_of(jp * 2 * groups, 2 * groups), 2 * groups)
        x_real[:, at, :] = jnp.concatenate(reals, axis=1).astype(jnp.bfloat16)
        x_imag[:, at, :] = jnp.concatenate(imags, axis=1).astype(jnp.bfloat16)

    @pl.loop(0, n_chan // 4)
    def _(q):
        real = jnp.concatenate([x_real[2 * q], x_real[2 * q + 1]], axis=1)
        imag = jnp.concatenate([x_imag[2 * q], x_imag[2 * q + 1]], axis=1)
        lagged = jnp.dot(table_ref[0], real, preferred_element_type=jnp.float32)
        lagged += jnp.dot(table_ref[1], imag, preferred_element_type=jnp.float32)
        turned = (lagged * lag_scale).T.astype(jnp.bfloat16)
        out_ref[pl.ds(q * 4, 4)] = turned.reshape(4, n_src, n_lags)


def correlate(receivers, source, table, lag_scale, groups):
    n_chan, depth, lanes = receivers.shape
    n_src = source.shape[0]
    n_lags, n_freqs = table.shape[1:]
    chunk = n_chan // CHUNKS
    bf16 = jnp.bfloat16
    return pl.pallas_call(
        functools.partial(correlate_kernel, lag_scale, groups),
        grid=(CHUNKS,),
        out_shape=jax.ShapeDtypeStruct((n_chan, n_src, n_lags), bf16),
        in_specs=[
            pl.BlockSpec((chunk, depth, lanes), lambda c: (c, 0, 0)),
            pl.BlockSpec((n_src, depth, lanes), lambda c: (0, 0, 0)),
            pl.BlockSpec((2, n_lags, n_freqs), lambda c: (0, 0, 0)),
        ],
        out_specs=pl.BlockSpec((chunk, n_src, n_lags), lambda c: (c, 0, 0)),
        scratch_shapes=[
            pltpu.VMEM((depth // LANES, n_src * lanes, LANES), jnp.float32),
            pltpu.VMEM((lanes, 2 * n_src, depth), bf16),
            pltpu.VMEM((chunk // 2, n_freqs, 2 * n_src), bf16),
            pltpu.VMEM((chunk // 2, n_freqs, 2 * n_src), bf16),
        ],
        compiler_params=pltpu.CompilerParams(vmem_limit_bytes=56 << 20),
        name="correlate",
    )(receivers, source, table)


def body(n_win, n_rcv, spectra, source_block):
    n_chan, n_time, parts, n_freqs = spectra.shape
    groups = n_freqs // LANES
    lag_scale = 1.0 / math.sqrt(2 * n_freqs * n_time * n_win)
    tables = jnp.asarray(lag_table(n_freqs, n_win, groups))
    table = lax.dynamic_index_in_dim(tables, lax.axis_index("win"), 0, keepdims=False)
    own = spectra.reshape(n_chan, n_time * parts * groups, LANES)
    receivers, source = gather(source_block, own, n_win, n_rcv)
    return correlate(receivers, source, table, lag_scale, groups)


def solution(mesh):
    in_specs = (P("rcv", "win", None, None), P())
    out_specs = P("rcv", None, "win")
    fn = functools.partial(body, mesh.shape["win"], mesh.shape["rcv"])
    return jax.shard_map(fn, mesh=mesh, in_specs=in_specs, out_specs=out_specs, check_vma=False)
```

```python
import functools
import math

import jax
import jax.numpy as jnp
import ml_dtypes
import numpy as np
from jax import lax
from jax.experimental import pallas as pl
from jax.experimental.pallas import tpu as pltpu
from jax.sharding import PartitionSpec as P

MESH = pl.DeviceIdType.MESH
LANES = 128
CHUNKS = 4


def lag_table(n_freqs, n_win, groups):
    n_lags = 2 * n_freqs
    column = np.arange(n_freqs)
    freq = (column % groups) * LANES + column // groups
    lag = (np.arange(n_lags) - n_freqs).reshape(n_win, 1, n_lags // n_win, 1)
    angle = (2.0 * math.pi / n_lags) * ((freq * lag) % n_lags)
    table = np.concatenate([np.cos(angle), -np.sin(angle)], axis=1)
    return table.astype(ml_dtypes.bfloat16)


def store_turned(flipped, row, block):
    turned = block.astype(jnp.float32).T
    at = pl.ds(pl.multiple_of(row * LANES, LANES), LANES)
    for slab in range(flipped.shape[0]):
        flipped[slab, at, :] = turned[:, slab * LANES:(slab + 1) * LANES]


def load_turned(flipped, j, count):
    slabs = [flipped[slab, pl.ds(j, count, stride=LANES), :] for slab in range(flipped.shape[0])]
    return jnp.concatenate(slabs, axis=1)


def prepare_source(groups, s_ref, flipped, weights):
    n_src, depth, _ = s_ref.shape

    @pl.loop(0, n_src)
    def _(s):
        store_turned(flipped, s, s_ref[s])

    lane = lax.broadcasted_iota(jnp.int32, (1, depth), 1)
    is_real = lax.rem(lane, 2 * groups) < groups

    @pl.loop(0, LANES)
    def _(j):
        spec = load_turned(flipped, j, n_src)
        turned = jnp.where(is_real, pltpu.roll(spec, depth - groups, 1), -pltpu.roll(spec, groups, 1))
        weights[j, :, :2 * n_src] = jnp.concatenate([spec, spec], axis=0).T.astype(jnp.bfloat16)
        weights[j, :, 2 * n_src:] = jnp.concatenate([turned, turned], axis=0).T.astype(jnp.bfloat16)


def turn_receivers(first, count, r_ref, flipped):
    @pl.loop(0, count)
    def _(r):
        store_turned(flipped, r, r_ref[first + r])


def cross_part(first, last, groups, n_chan, flipped, weights, x_real, x_imag):
    depth, n_src = weights.shape[1], weights.shape[2] // 4
    row = lax.broadcasted_iota(jnp.int32, (groups, depth), 0)
    picked = (lax.rem(lax.broadcasted_iota(jnp.int32, (groups, depth), 1), groups) == row)[None]
    first_half = lax.broadcasted_iota(jnp.int32, (1, 1, 2 * n_src), 2) < n_src

    @pl.loop(first, last)
    def _(jp):
        reals, imags = [], []
        for k in range(2):
            j = 2 * jp + k
            spec = load_turned(flipped, j, n_chan)
            spread = jnp.where(picked, spec[:, None, :], 0.0).reshape(n_chan * groups, depth).astype(jnp.bfloat16)
            cross = jnp.dot(spread, weights[j], preferred_element_type=jnp.float32)
            for half, kept in ((0, reals), (1, imags)):
                part = cross[:, half * 2 * n_src:(half + 1) * 2 * n_src].reshape(n_chan // 2, 2, groups, 2 * n_src)
                kept.append(jnp.where(first_half, part[:, 0], part[:, 1]))
        at = pl.ds(pl.multiple_of(jp * 2 * groups, 2 * groups), 2 * groups)
        x_real[:, at, :] = jnp.concatenate(reals, axis=1).astype(jnp.bfloat16)
        x_imag[:, at, :] = jnp.concatenate(imags, axis=1).astype(jnp.bfloat16)


def lags_of(first, n_chan, lag_scale, table_ref, x_real, x_imag, out_ref):
    n_src, n_lags = out_ref.shape[1:]

    @pl.loop(0, n_chan // 4)
    def _(q):
        real = jnp.concatenate([x_real[2 * q], x_real[2 * q + 1]], axis=1)
        imag = jnp.concatenate([x_imag[2 * q], x_imag[2 * q + 1]], axis=1)
        lagged = jnp.dot(table_ref[0], real, preferred_element_type=jnp.float32)
        lagged += jnp.dot(table_ref[1], imag, preferred_element_type=jnp.float32)
        turned = (lagged * lag_scale).T.astype(jnp.bfloat16)
        out_ref[pl.ds(first + q * 4, 4)] = turned.reshape(4, n_src, n_lags)


def fused_kernel(n_win, n_rcv, groups, lag_scale, root_ref, own_ref, table_ref, out_ref, recv_out, src_out, slots,
                 flipped, weights, x_real, x_imag, sp_send, sp_recv, r_send, r_recv, z_send, z_recv, x_send, x_recv,
                 c_send, c_recv, local_sem):
    me_w = lax.axis_index("win")
    me_r = lax.axis_index("rcv")
    n_chan, rows = own_ref.shape[0], own_ref.shape[1]
    part = n_chan // n_rcv
    chunk = n_chan // CHUNKS
    sibling = me_r + 1 - 2 * lax.rem(me_r, 2)
    n_chip = n_rcv // 2

    barrier = pltpu.get_barrier_semaphore()

    @pl.when(me_w > 0)
    def _():
        pl.semaphore_signal(barrier, inc=1, device_id=(me_w - 1, me_r), device_id_type=MESH)

    @pl.when(me_w < n_win - 1)
    def _():
        pl.semaphore_signal(barrier, inc=1, device_id=(me_w + 1, me_r), device_id_type=MESH)

    @pl.loop(1, n_rcv)
    def _(d):
        pl.semaphore_signal(barrier, inc=1, device_id=(me_w, lax.rem(me_r + d, n_rcv)), device_id_type=MESH)

    on_line = (me_w > 0).astype(jnp.int32) + (me_w < n_win - 1).astype(jnp.int32)
    pl.semaphore_wait(barrier, n_rcv - 1 + on_line)

    def piece_copy(d):
        target = lax.rem(me_r + d, n_rcv)
        return pltpu.make_async_remote_copy(
            src_ref=own_ref.at[pl.ds(target * part, part)], dst_ref=slots.at[me_r],
            send_sem=sp_send.at[d], recv_sem=sp_recv.at[d],
            device_id=(me_w, target), device_id_type=MESH)

    def hop(buffer, first, count, origin, send_sem, recv_sem, step):
        block = buffer.at[pl.ds(first, count), pl.ds(origin * rows, rows), :]
        return pltpu.make_async_remote_copy(
            src_ref=block, dst_ref=block, send_sem=send_sem, recv_sem=recv_sem,
            device_id=(me_w + step, me_r), device_id_type=MESH)

    def recv_hop(c, t, way):
        step = 1 - 2 * way
        return hop(recv_out, c * chunk, chunk, me_w - step * t, r_send.at[way, t, c], r_recv.at[way, t, c], step)

    def src_hop(t, way):
        step = 1 - 2 * way
        return hop(src_out, me_r * part, part, me_w - step * t, z_send.at[way, t], z_recv.at[way, t], step)

    def can_send(t, way):
        return (me_w >= t) & (me_w < n_win - 1) if way == 0 else (me_w + t < n_win) & (me_w > 0)

    def can_receive(t, way):
        return me_w > t if way == 0 else me_w + t + 1 < n_win


    def recv_arrival(c, t, way):
        step = 1 - 2 * way
        return hop(recv_out, c * chunk, chunk, me_w - step * (t + 1), r_send.at[way, t, c], r_recv.at[way, t, c], 0)

    def src_arrival(t, way):
        step = 1 - 2 * way
        return hop(src_out, me_r * part, part, me_w - step * (t + 1), z_send.at[way, t], z_recv.at[way, t], 0)

    @pl.loop(1, n_rcv)
    def _(d):
        piece_copy(d).start()

    own_local = pltpu.make_async_copy(own_ref, recv_out.at[:, pl.ds(me_w * rows, rows), :], local_sem.at[0])
    own_local.start()
    piece_local = pltpu.make_async_copy(own_ref.at[pl.ds(me_r * part, part)], slots.at[me_r], local_sem.at[1])
    piece_local.start()
    own_local.wait()

    def start_own(c):
        for way in range(2):
            @pl.when(can_send(0, way))
            def _():
                recv_hop(c, 0, way).start()

    start_own(0)
    start_own(1)

    piece_local.wait()

    @pl.loop(1, n_rcv)
    def _(d):
        piece_copy(d).wait()

    mine = (pl.ds(me_r * part, part), pl.ds(pl.multiple_of(me_w * rows, rows), rows), slice(None))
    src_out[mine] = slots[root_ref[0]]
    for way in range(2):
        @pl.when(can_send(0, way))
        def _():
            src_hop(0, way).start()
    for c in range(2, CHUNKS):
        start_own(c)
    for t in range(n_win - 1):
        for way in range(2):
            @pl.when(can_receive(t, way))
            def _():
                src_arrival(t, way).wait_recv()

            @pl.when(can_send(t + 1, way))
            def _():
                src_hop(t + 1, way).start()

    def block_copy(owner, target, send_sem, recv_sem):
        block = src_out.at[pl.ds(owner * part, part)]
        return pltpu.make_async_remote_copy(
            src_ref=block, dst_ref=block, send_sem=send_sem, recv_sem=recv_sem,
            device_id=(me_w, target), device_id_type=MESH)

    def chip_copy(d):
        return block_copy(me_r, lax.rem(me_r + 2 * d, n_rcv), x_send.at[d], x_recv.at[d])

    def core_copy(d):
        return block_copy(lax.rem(me_r - 2 * d + n_rcv, n_rcv), sibling, c_send.at[d], c_recv.at[d])

    def core_arrival(d):
        return block_copy(lax.rem(sibling - 2 * d + n_rcv, n_rcv), sibling, c_send.at[d], c_recv.at[d])

    def chip_arrival(d):
        return block_copy(lax.rem(me_r - 2 * d + n_rcv, n_rcv), sibling, x_send.at[d], x_recv.at[d])

    @pl.loop(1, n_chip)
    def _(d):
        chip_copy(d).start()

    core_copy(0).start()

    def forward(c, t):
        for way in range(2):
            @pl.when(can_receive(t, way))
            def _():
                recv_arrival(c, t, way).wait_recv()

            @pl.when(can_send(t + 1, way))
            def _():
                recv_hop(c, t + 1, way).start()

    for t in range(n_win - 1):
        forward(0, t)

    @pl.loop(1, n_chip)
    def _(d):
        chip_arrival(d).wait_recv()
        core_copy(d).start()

    forward(1, 0)

    @pl.loop(0, n_chip)
    def _(d):
        core_arrival(d).wait_recv()

    prepare_source(groups, src_out, flipped, weights)

    pairs = LANES // 2
    cuts = [pairs * t // n_win for t in range(n_win + 1)]

    def compute(c, ahead):
        turn_receivers(c * chunk, chunk, recv_out, flipped)
        for t in range(n_win):
            cross_part(cuts[t], cuts[t + 1], groups, chunk, flipped, weights, x_real, x_imag)
            if ahead and t < n_win - 1:
                forward(c + 1, t)
        lags_of(c * chunk, chunk, lag_scale, table_ref, x_real, x_imag, out_ref)

    def compute_first():
        turn_receivers(0, chunk, recv_out, flipped)
        for t in range(n_win):
            cross_part(cuts[t], cuts[t + 1], groups, chunk, flipped, weights, x_real, x_imag)
            if 0 < t < n_win - 1:
                forward(1, t)
        lags_of(0, chunk, lag_scale, table_ref, x_real, x_imag, out_ref)

    compute_first()

    @pl.loop(1, CHUNKS - 1)
    def _(c):
        compute(c, True)

    compute(CHUNKS - 1, False)

    @pl.loop(0, n_chip)
    def _(d):
        core_copy(d).wait_send()

    @pl.loop(1, n_chip)
    def _(d):
        chip_copy(d).wait_send()

    for t in range(n_win - 1):
        for way in range(2):
            @pl.when(can_send(t, way))
            def _():
                src_hop(t, way).wait_send()
                for c in range(CHUNKS):
                    recv_hop(c, t, way).wait_send()


def fused(root, own, table, n_win, n_rcv, lag_scale, groups):
    n_chan, rows, lanes = own.shape
    part = n_chan // n_rcv
    chunk = n_chan // CHUNKS
    depth = n_win * rows
    n_lags, n_freqs = table.shape[1:]
    bf16 = own.dtype
    sem = pltpu.SemaphoreType.DMA
    return pl.pallas_call(
        functools.partial(fused_kernel, n_win, n_rcv, groups, lag_scale),
        out_shape=jax.ShapeDtypeStruct((n_chan, n_chan, n_lags), bf16),
        in_specs=[
            pl.BlockSpec(memory_space=pltpu.SMEM),
            pl.BlockSpec(memory_space=pl.ANY),
            pl.BlockSpec(memory_space=pltpu.VMEM),
        ],
        out_specs=pl.BlockSpec(memory_space=pltpu.VMEM),
        scratch_shapes=[
            pltpu.VMEM((n_chan, depth, lanes), bf16),
            pltpu.VMEM((n_chan, depth, lanes), bf16),
            pltpu.VMEM((n_rcv, part, rows, lanes), bf16),
            pltpu.VMEM((depth // LANES, n_chan * lanes, LANES), jnp.float32),
            pltpu.VMEM((lanes, depth, 4 * n_chan), bf16),
            pltpu.VMEM((chunk // 2, n_freqs, 2 * n_chan), bf16),
            pltpu.VMEM((chunk // 2, n_freqs, 2 * n_chan), bf16),
            sem((n_rcv,)), sem((n_rcv,)),
            sem((2, n_win, CHUNKS)), sem((2, n_win, CHUNKS)),
            sem((2, n_win)), sem((2, n_win)),
            sem((n_rcv,)), sem((n_rcv,)),
            sem((n_rcv,)), sem((n_rcv,)),
            sem((2,)),
        ],
        compiler_params=pltpu.CompilerParams(
            collective_id=0, has_side_effects=True, vmem_limit_bytes=56 << 20),
        name="fused",
    )(root, own, table)


def body(n_win, n_rcv, spectra, source_block):
    n_chan, n_time, parts, n_freqs = spectra.shape
    groups = n_freqs // LANES
    lag_scale = 1.0 / math.sqrt(2 * n_freqs * n_time * n_win)
    tables = jnp.asarray(lag_table(n_freqs, n_win, groups))
    table = lax.dynamic_index_in_dim(tables, lax.axis_index("win"), 0, keepdims=False)
    own = spectra.reshape(n_chan, n_time * parts * groups, LANES)
    return fused(source_block, own, table, n_win, n_rcv, lag_scale, groups)


def solution(mesh):
    in_specs = (P("rcv", "win", None, None), P())
    out_specs = P("rcv", None, "win")
    fn = functools.partial(body, mesh.shape["win"], mesh.shape["rcv"])
    return jax.shard_map(fn, mesh=mesh, in_specs=in_specs, out_specs=out_specs, check_vma=False)
```

```python
import functools
import math

import jax
import jax.numpy as jnp
import ml_dtypes
import numpy as np
from jax import lax
from jax.experimental import pallas as pl
from jax.experimental.pallas import tpu as pltpu
from jax.sharding import PartitionSpec as P

MESH = pl.DeviceIdType.MESH
LANES = 128
CHUNKS = 4


def lag_table(n_freqs, n_win, groups):
    n_lags = 2 * n_freqs
    column = np.arange(n_freqs)
    freq = (column % groups) * LANES + column // groups
    lag = (np.arange(n_lags) - n_freqs).reshape(n_win, 1, n_lags // n_win, 1)
    angle = (2.0 * math.pi / n_lags) * ((freq * lag) % n_lags)
    table = np.concatenate([np.cos(angle), -np.sin(angle)], axis=1)
    return table.astype(ml_dtypes.bfloat16)


def store_turned(flipped, row, block):
    turned = block.astype(jnp.float32).T
    at = pl.ds(pl.multiple_of(row * LANES, LANES), LANES)
    for slab in range(flipped.shape[0]):
        flipped[slab, at, :] = turned[:, slab * LANES:(slab + 1) * LANES]


def load_turned(flipped, j, count):
    slabs = [flipped[slab, pl.ds(j, count, stride=LANES), :] for slab in range(flipped.shape[0])]
    return jnp.concatenate(slabs, axis=1)


def prepare_source(groups, s_ref, flipped, weights):
    n_src, depth, _ = s_ref.shape

    @pl.loop(0, n_src)
    def _(s):
        store_turned(flipped, s, s_ref[s])

    first_half = lax.broadcasted_iota(jnp.int32, (1, 2 * n_src), 1) < n_src

    @pl.loop(0, LANES // 2)
    def _(jp):
        both = jnp.concatenate([load_turned(flipped, 2 * jp, n_src), load_turned(flipped, 2 * jp + 1, n_src)], axis=0).T
        crossed = pltpu.roll(both, n_src, 1)
        for k, (low, high) in enumerate(((both, crossed), (crossed, both))):
            real = jnp.where(first_half, low, high)
            pairs = real.reshape(depth // (2 * groups), 2, groups, 2 * n_src)
            imag = jnp.stack([pairs[:, 1], -pairs[:, 0]], axis=1).reshape(depth, 2 * n_src)
            weights[2 * jp + k, :, :2 * n_src] = real.astype(jnp.bfloat16)
            weights[2 * jp + k, :, 2 * n_src:] = imag.astype(jnp.bfloat16)


def turn_receivers(first, count, r_ref, flipped):
    @pl.loop(0, count)
    def _(r):
        store_turned(flipped, r, r_ref[first + r])


def cross_part(first, last, groups, n_chan, flipped, weights, x_real, x_imag):
    depth, n_src = weights.shape[1], weights.shape[2] // 4
    row = lax.broadcasted_iota(jnp.int32, (groups, LANES), 0)
    picked = lax.rem(lax.broadcasted_iota(jnp.int32, (groups, LANES), 1), groups) == row
    first_half = lax.broadcasted_iota(jnp.int32, (1, 1, 2 * n_src), 2) < n_src

    @pl.loop(first, last)
    def _(jp):
        reals, imags = [], []
        for k in range(2):
            j = 2 * jp + k
            slabs = []
            for slab in range(depth // LANES):
                rows = [jnp.where(picked, flipped[slab, pl.ds(r * LANES + j, 1), :], 0.0) for r in range(n_chan)]
                slabs.append(jnp.concatenate(rows, axis=0).astype(jnp.bfloat16))
            spread = jnp.concatenate(slabs, axis=1)
            cross = jnp.dot(spread, weights[j], preferred_element_type=jnp.float32)
            for half, kept in ((0, reals), (1, imags)):
                part = cross[:, half * 2 * n_src:(half + 1) * 2 * n_src].reshape(n_chan // 2, 2, groups, 2 * n_src)
                kept.append(jnp.where(first_half, part[:, 0], part[:, 1]))
        at = pl.ds(pl.multiple_of(jp * 2 * groups, 2 * groups), 2 * groups)
        x_real[:, at, :] = jnp.concatenate(reals, axis=1).astype(jnp.bfloat16)
        x_imag[:, at, :] = jnp.concatenate(imags, axis=1).astype(jnp.bfloat16)


def lags_of(first, n_chan, lag_scale, table_ref, x_real, x_imag, out_ref):
    n_src, n_lags = out_ref.shape[1:]

    @pl.loop(0, n_chan // 4)
    def _(q):
        real = jnp.concatenate([x_real[2 * q], x_real[2 * q + 1]], axis=1)
        imag = jnp.concatenate([x_imag[2 * q], x_imag[2 * q + 1]], axis=1)
        lagged = jnp.dot(table_ref[0], real, preferred_element_type=jnp.float32)
        lagged += jnp.dot(table_ref[1], imag, preferred_element_type=jnp.float32)
        turned = (lagged * lag_scale).T.astype(jnp.bfloat16)
        out_ref[pl.ds(first + q * 4, 4)] = turned.reshape(4, n_src, n_lags)


def fused_kernel(n_win, n_rcv, groups, lag_scale, root_ref, own_ref, table_ref, out_ref, recv_out, src_out, slots,
                 flipped, weights, x_real, x_imag, sp_send, sp_recv, r_send, r_recv, z_send, z_recv, x_send, x_recv,
                 c_send, c_recv, local_sem):
    me_w = lax.axis_index("win")
    me_r = lax.axis_index("rcv")
    n_chan, rows = own_ref.shape[0], own_ref.shape[1]
    part = n_chan // n_rcv
    chunk = n_chan // CHUNKS
    sibling = me_r + 1 - 2 * lax.rem(me_r, 2)
    n_chip = n_rcv // 2

    barrier = pltpu.get_barrier_semaphore()

    @pl.when(me_w > 0)
    def _():
        pl.semaphore_signal(barrier, inc=1, device_id=(me_w - 1, me_r), device_id_type=MESH)

    @pl.when(me_w < n_win - 1)
    def _():
        pl.semaphore_signal(barrier, inc=1, device_id=(me_w + 1, me_r), device_id_type=MESH)

    @pl.loop(1, n_rcv)
    def _(d):
        pl.semaphore_signal(barrier, inc=1, device_id=(me_w, lax.rem(me_r + d, n_rcv)), device_id_type=MESH)

    on_line = (me_w > 0).astype(jnp.int32) + (me_w < n_win - 1).astype(jnp.int32)
    pl.semaphore_wait(barrier, n_rcv - 1 + on_line)

    def piece_copy(d):
        target = lax.rem(me_r + d, n_rcv)
        return pltpu.make_async_remote_copy(
            src_ref=own_ref.at[pl.ds(target * part, part)], dst_ref=slots.at[me_r],
            send_sem=sp_send.at[d], recv_sem=sp_recv.at[d],
            device_id=(me_w, target), device_id_type=MESH)

    def hop(buffer, first, count, origin, send_sem, recv_sem, step):
        block = buffer.at[pl.ds(first, count), pl.ds(origin * rows, rows), :]
        return pltpu.make_async_remote_copy(
            src_ref=block, dst_ref=block, send_sem=send_sem, recv_sem=recv_sem,
            device_id=(me_w + step, me_r), device_id_type=MESH)

    def recv_hop(c, t, way):
        step = 1 - 2 * way
        return hop(recv_out, c * chunk, chunk, me_w - step * t, r_send.at[way, t, c], r_recv.at[way, t, c], step)

    def src_hop(t, way):
        step = 1 - 2 * way
        return hop(src_out, me_r * part, part, me_w - step * t, z_send.at[way, t], z_recv.at[way, t], step)

    def can_send(t, way):
        return (me_w >= t) & (me_w < n_win - 1) if way == 0 else (me_w + t < n_win) & (me_w > 0)

    def can_receive(t, way):
        return me_w > t if way == 0 else me_w + t + 1 < n_win


    def recv_arrival(c, t, way):
        step = 1 - 2 * way
        return hop(recv_out, c * chunk, chunk, me_w - step * (t + 1), r_send.at[way, t, c], r_recv.at[way, t, c], 0)

    def src_arrival(t, way):
        step = 1 - 2 * way
        return hop(src_out, me_r * part, part, me_w - step * (t + 1), z_send.at[way, t], z_recv.at[way, t], 0)

    @pl.loop(1, n_rcv)
    def _(d):
        piece_copy(d).start()

    own_local = pltpu.make_async_copy(own_ref, recv_out.at[:, pl.ds(me_w * rows, rows), :], local_sem.at[0])
    own_local.start()
    piece_local = pltpu.make_async_copy(own_ref.at[pl.ds(me_r * part, part)], slots.at[me_r], local_sem.at[1])
    piece_local.start()
    own_local.wait()

    def start_own(c):
        for way in range(2):
            @pl.when(can_send(0, way))
            def _():
                recv_hop(c, 0, way).start()

    start_own(0)
    start_own(1)

    piece_local.wait()

    @pl.loop(1, n_rcv)
    def _(d):
        piece_copy(d).wait()

    mine = (pl.ds(me_r * part, part), pl.ds(pl.multiple_of(me_w * rows, rows), rows), slice(None))
    src_out[mine] = slots[root_ref[0]]
    for way in range(2):
        @pl.when(can_send(0, way))
        def _():
            src_hop(0, way).start()
    def block_copy(owner, origin, target, send_sem, recv_sem):
        block = src_out.at[pl.ds(owner * part, part), pl.ds(pl.multiple_of(origin * rows, rows), rows), :]
        return pltpu.make_async_remote_copy(
            src_ref=block, dst_ref=block, send_sem=send_sem, recv_sem=recv_sem,
            device_id=(me_w, target), device_id_type=MESH)

    def chip_copy(w, d):
        return block_copy(me_r, w, lax.rem(me_r + 2 * d, n_rcv), x_send.at[w, d], x_recv.at[w, d])

    def chip_arrival(w, d):
        return block_copy(lax.rem(me_r - 2 * d + n_rcv, n_rcv), w, sibling, x_send.at[w, d], x_recv.at[w, d])

    def core_copy(w, d):
        return block_copy(lax.rem(me_r - 2 * d + n_rcv, n_rcv), w, sibling, c_send.at[w, d], c_recv.at[w, d])

    def core_arrival(w, d):
        return block_copy(lax.rem(sibling - 2 * d + n_rcv, n_rcv), w, sibling, c_send.at[w, d], c_recv.at[w, d])

    def spread_block(w):
        @pl.loop(1, n_chip)
        def _(d):
            chip_copy(w, d).start()

        core_copy(w, 0).start()

    spread_block(me_w)
    for t in range(n_win - 1):
        for way in range(2):
            @pl.when(can_receive(t, way))
            def _():
                src_arrival(t, way).wait_recv()

            @pl.when(can_send(t + 1, way))
            def _():
                src_hop(t + 1, way).start()

            @pl.when(can_receive(t, way))
            def _():
                spread_block(me_w - (1 - 2 * way) * (t + 1))

    for c in range(2, CHUNKS):
        start_own(c)

    def forward(c, t):
        for way in range(2):
            @pl.when(can_receive(t, way))
            def _():
                recv_arrival(c, t, way).wait_recv()

            @pl.when(can_send(t + 1, way))
            def _():
                recv_hop(c, t + 1, way).start()

    for t in range(n_win - 1):
        forward(0, t)

    @pl.loop(0, n_win)
    def _(w):
        @pl.loop(1, n_chip)
        def _(d):
            chip_arrival(w, d).wait_recv()
            core_copy(w, d).start()

    forward(1, 0)

    @pl.loop(0, n_win)
    def _(w):
        @pl.loop(0, n_chip)
        def _(d):
            core_arrival(w, d).wait_recv()

    prepare_source(groups, src_out, flipped, weights)

    pairs = LANES // 2
    cuts = [pairs * t // n_win for t in range(n_win + 1)]

    def compute(c, ahead):
        turn_receivers(c * chunk, chunk, recv_out, flipped)
        for t in range(n_win):
            cross_part(cuts[t], cuts[t + 1], groups, chunk, flipped, weights, x_real, x_imag)
            if ahead and t < n_win - 1:
                forward(c + 1, t)
        lags_of(c * chunk, chunk, lag_scale, table_ref, x_real, x_imag, out_ref)

    def compute_first():
        turn_receivers(0, chunk, recv_out, flipped)
        for t in range(n_win):
            cross_part(cuts[t], cuts[t + 1], groups, chunk, flipped, weights, x_real, x_imag)
            if 0 < t < n_win - 1:
                forward(1, t)
        lags_of(0, chunk, lag_scale, table_ref, x_real, x_imag, out_ref)

    compute_first()

    @pl.loop(1, CHUNKS - 1)
    def _(c):
        compute(c, True)

    compute(CHUNKS - 1, False)

    @pl.loop(0, n_win)
    def _(w):
        @pl.loop(0, n_chip)
        def _(d):
            core_copy(w, d).wait_send()

        @pl.loop(1, n_chip)
        def _(d):
            chip_copy(w, d).wait_send()

    for t in range(n_win - 1):
        for way in range(2):
            @pl.when(can_send(t, way))
            def _():
                src_hop(t, way).wait_send()
                for c in range(CHUNKS):
                    recv_hop(c, t, way).wait_send()


def fused(root, own, table, n_win, n_rcv, lag_scale, groups):
    n_chan, rows, lanes = own.shape
    part = n_chan // n_rcv
    chunk = n_chan // CHUNKS
    depth = n_win * rows
    n_lags, n_freqs = table.shape[1:]
    bf16 = own.dtype
    sem = pltpu.SemaphoreType.DMA
    return pl.pallas_call(
        functools.partial(fused_kernel, n_win, n_rcv, groups, lag_scale),
        out_shape=jax.ShapeDtypeStruct((n_chan, n_chan, n_lags), bf16),
        in_specs=[
            pl.BlockSpec(memory_space=pltpu.SMEM),
            pl.BlockSpec(memory_space=pl.ANY),
            pl.BlockSpec(memory_space=pltpu.VMEM),
        ],
        out_specs=pl.BlockSpec(memory_space=pltpu.VMEM),
        scratch_shapes=[
            pltpu.VMEM((n_chan, depth, lanes), bf16),
            pltpu.VMEM((n_chan, depth, lanes), bf16),
            pltpu.VMEM((n_rcv, part, rows, lanes), bf16),
            pltpu.VMEM((depth // LANES, n_chan * lanes, LANES), jnp.float32),
            pltpu.VMEM((lanes, depth, 4 * n_chan), bf16),
            pltpu.VMEM((chunk // 2, n_freqs, 2 * n_chan), bf16),
            pltpu.VMEM((chunk // 2, n_freqs, 2 * n_chan), bf16),
            sem((n_rcv,)), sem((n_rcv,)),
            sem((2, n_win, CHUNKS)), sem((2, n_win, CHUNKS)),
            sem((2, n_win)), sem((2, n_win)),
            sem((n_win, n_rcv)), sem((n_win, n_rcv)),
            sem((n_win, n_rcv)), sem((n_win, n_rcv)),
            sem((2,)),
        ],
        compiler_params=pltpu.CompilerParams(
            collective_id=0, has_side_effects=True, vmem_limit_bytes=56 << 20),
        name="fused",
    )(root, own, table)


def body(n_win, n_rcv, spectra, source_block):
    n_chan, n_time, parts, n_freqs = spectra.shape
    groups = n_freqs // LANES
    lag_scale = 1.0 / math.sqrt(2 * n_freqs * n_time * n_win)
    tables = jnp.asarray(lag_table(n_freqs, n_win, groups))
    table = lax.dynamic_index_in_dim(tables, lax.axis_index("win"), 0, keepdims=False)
    own = spectra.reshape(n_chan, n_time * parts * groups, LANES)
    return fused(source_block, own, table, n_win, n_rcv, lag_scale, groups)


def solution(mesh):
    in_specs = (P("rcv", "win", None, None), P())
    out_specs = P("rcv", None, "win")
    fn = functools.partial(body, mesh.shape["win"], mesh.shape["rcv"])
    return jax.shard_map(fn, mesh=mesh, in_specs=in_specs, out_specs=out_specs, check_vma=False)
```

```python
import functools
import math

import jax
import jax.numpy as jnp
import ml_dtypes
import numpy as np
from jax import lax
from jax.experimental import pallas as pl
from jax.experimental.pallas import tpu as pltpu
from jax.sharding import PartitionSpec as P

MESH = pl.DeviceIdType.MESH
LANES = 128
CHUNKS = 4
HALVES = 2


def lag_table(n_freqs, n_win, groups):
    n_lags = 2 * n_freqs
    column = np.arange(n_freqs)
    freq = (column % groups) * LANES + column // groups
    lag = (np.arange(n_lags) - n_freqs).reshape(n_win, 1, n_lags // n_win, 1)
    angle = (2.0 * math.pi / n_lags) * ((freq * lag) % n_lags)
    table = np.concatenate([np.cos(angle), -np.sin(angle)], axis=1)
    slabs = table.reshape(n_win, 2, n_lags // n_win, groups, LANES).swapaxes(2, 3)
    return np.ascontiguousarray(slabs).astype(ml_dtypes.bfloat16)


def store_turned(flipped, row, block):
    turned = block.astype(jnp.float32).T
    at = pl.ds(pl.multiple_of(row * LANES, LANES), LANES)
    for slab in range(flipped.shape[0]):
        flipped[slab, at, :] = turned[:, slab * LANES:(slab + 1) * LANES]


def load_turned(flipped, j, count):
    slabs = [flipped[slab, pl.ds(j, count, stride=LANES), :] for slab in range(flipped.shape[0])]
    return jnp.concatenate(slabs, axis=1)


def prepare_source(groups, s_ref, flipped, weights):
    n_src, depth, _ = s_ref.shape

    @pl.loop(0, n_src, unroll=4)
    def _(s):
        store_turned(flipped, s, s_ref[s])

    first_half = lax.broadcasted_iota(jnp.int32, (1, 2 * n_src), 1) < n_src

    @pl.loop(0, LANES // 2, unroll=2)
    def _(jp):
        both = jnp.concatenate([load_turned(flipped, 2 * jp, n_src), load_turned(flipped, 2 * jp + 1, n_src)], axis=0).T
        crossed = pltpu.roll(both, n_src, 1)
        for k, (low, high) in enumerate(((both, crossed), (crossed, both))):
            real = jnp.where(first_half, low, high)
            pairs = real.reshape(depth // (2 * groups), 2, groups, 2 * n_src)
            imag = jnp.stack([pairs[:, 1], -pairs[:, 0]], axis=1).reshape(depth, 2 * n_src)
            weights[2 * jp + k, :, :2 * n_src] = real.astype(jnp.bfloat16)
            weights[2 * jp + k, :, 2 * n_src:] = imag.astype(jnp.bfloat16)


def turn_receivers(first, count, r_ref, flipped):
    @pl.loop(0, count, unroll=4)
    def _(r):
        store_turned(flipped, r, r_ref[first + r])


def cross_part(first, last, groups, n_chan, flipped, weights, x_real, x_imag):
    depth, n_src = weights.shape[1], weights.shape[2] // 4
    row = lax.broadcasted_iota(jnp.int32, (groups, LANES), 0)
    picked = lax.rem(lax.broadcasted_iota(jnp.int32, (groups, LANES), 1), groups) == row
    first_half = lax.broadcasted_iota(jnp.int32, (1, 1, 2 * n_src), 2) < n_src

    @pl.loop(first, last, unroll=2)
    def _(jp):
        reals, imags = [], []
        for k in range(2):
            j = 2 * jp + k
            slabs = []
            for slab in range(depth // LANES):
                rows = [jnp.where(picked, flipped[slab, pl.ds(r * LANES + j, 1), :], 0.0) for r in range(n_chan)]
                slabs.append(jnp.concatenate(rows, axis=0).astype(jnp.bfloat16))
            spread = jnp.concatenate(slabs, axis=1)
            cross = jnp.dot(spread, weights[j], preferred_element_type=jnp.float32)
            for half, kept in ((0, reals), (1, imags)):
                part = cross[:, half * 2 * n_src:(half + 1) * 2 * n_src].reshape(n_chan // 2, 2, groups, 2 * n_src)
                kept.append(jnp.where(first_half, part[:, 0], part[:, 1]))
        at = pl.ds(pl.multiple_of(jp * 2 * groups, 2 * groups), 2 * groups)
        x_real[:, at, :] = jnp.concatenate(reals, axis=1).astype(jnp.bfloat16)
        x_imag[:, at, :] = jnp.concatenate(imags, axis=1).astype(jnp.bfloat16)


def lags_of(first, n_chan, lag_scale, table_ref, x_real, x_imag, out_ref):
    n_src, n_lags = out_ref.shape[1:]

    @pl.loop(0, n_chan // 4, unroll=2)
    def _(q):
        real = jnp.concatenate([x_real[2 * q], x_real[2 * q + 1]], axis=1)
        imag = jnp.concatenate([x_imag[2 * q], x_imag[2 * q + 1]], axis=1)
        cosines, sines = (jnp.concatenate([table_ref[p, k] for k in range(table_ref.shape[1])], axis=1) for p in range(2))
        lagged = jnp.dot(cosines, real, preferred_element_type=jnp.float32)
        lagged += jnp.dot(sines, imag, preferred_element_type=jnp.float32)
        turned = (lagged * lag_scale).T.astype(jnp.bfloat16)
        out_ref[pl.ds(first + q * 4, 4)] = turned.reshape(4, n_src, n_lags)


def fused_kernel(n_win, n_rcv, groups, lag_scale, root_ref, own_ref, table_ref, out_ref, recv_out, src_out, slots,
                 table, flipped, weights, x_real, x_imag, sp_send, sp_recv, r_send, r_recv, z_send, z_recv, x_send, x_recv,
                 c_send, c_recv, local_sem):
    me_w = lax.axis_index("win")
    me_r = lax.axis_index("rcv")
    n_chan, rows = own_ref.shape[0], own_ref.shape[1]
    part = n_chan // n_rcv
    chunk = n_chan // CHUNKS
    sibling = me_r + 1 - 2 * lax.rem(me_r, 2)
    n_chip = n_rcv // 2

    barrier = pltpu.get_barrier_semaphore()

    @pl.when(me_w > 0)
    def _():
        pl.semaphore_signal(barrier, inc=1, device_id=(me_w - 1, me_r), device_id_type=MESH)

    @pl.when(me_w < n_win - 1)
    def _():
        pl.semaphore_signal(barrier, inc=1, device_id=(me_w + 1, me_r), device_id_type=MESH)

    @pl.loop(1, n_rcv)
    def _(d):
        pl.semaphore_signal(barrier, inc=1, device_id=(me_w, lax.rem(me_r + d, n_rcv)), device_id_type=MESH)

    on_line = (me_w > 0).astype(jnp.int32) + (me_w < n_win - 1).astype(jnp.int32)
    pl.semaphore_wait(barrier, n_rcv - 1 + on_line)

    def piece_copy(d):
        target = lax.rem(me_r + d, n_rcv)
        return pltpu.make_async_remote_copy(
            src_ref=own_ref.at[pl.ds(target * part, part)], dst_ref=slots.at[me_r],
            send_sem=sp_send.at[d], recv_sem=sp_recv.at[d],
            device_id=(me_w, target), device_id_type=MESH)

    def hop(buffer, first, count, origin, send_sem, recv_sem, step):
        block = buffer.at[pl.ds(first, count), pl.ds(origin * rows, rows), :]
        return pltpu.make_async_remote_copy(
            src_ref=block, dst_ref=block, send_sem=send_sem, recv_sem=recv_sem,
            device_id=(me_w + step, me_r), device_id_type=MESH)

    def recv_hop(c, t, way):
        step = 1 - 2 * way
        return hop(recv_out, c * chunk, chunk, me_w - step * t, r_send.at[way, t, c], r_recv.at[way, t, c], step)

    def src_hop(t, way):
        step = 1 - 2 * way
        return hop(src_out, me_r * part, part, me_w - step * t, z_send.at[way, t], z_recv.at[way, t], step)

    def can_send(t, way):
        return (me_w >= t) & (me_w < n_win - 1) if way == 0 else (me_w + t < n_win) & (me_w > 0)

    def can_receive(t, way):
        return me_w > t if way == 0 else me_w + t + 1 < n_win


    def recv_arrival(c, t, way):
        step = 1 - 2 * way
        return hop(recv_out, c * chunk, chunk, me_w - step * (t + 1), r_send.at[way, t, c], r_recv.at[way, t, c], 0)

    def src_arrival(t, way):
        step = 1 - 2 * way
        return hop(src_out, me_r * part, part, me_w - step * (t + 1), z_send.at[way, t], z_recv.at[way, t], 0)

    @pl.loop(1, n_rcv)
    def _(d):
        piece_copy(d).start()

    table_local = pltpu.make_async_copy(table_ref.at[me_w], table, local_sem.at[2])
    table_local.start()
    own_local = pltpu.make_async_copy(own_ref, recv_out.at[:, pl.ds(me_w * rows, rows), :], local_sem.at[0])
    own_local.start()
    piece_local = pltpu.make_async_copy(own_ref.at[pl.ds(me_r * part, part)], slots.at[me_r], local_sem.at[1])
    piece_local.start()
    own_local.wait()

    def start_own(c):
        for way in range(2):
            @pl.when(can_send(0, way))
            def _():
                recv_hop(c, 0, way).start()

    start_own(0)
    start_own(1)

    piece_local.wait()

    @pl.loop(1, n_rcv)
    def _(d):
        piece_copy(d).wait()

    mine = (pl.ds(me_r * part, part), pl.ds(pl.multiple_of(me_w * rows, rows), rows), slice(None))
    src_out[mine] = slots[root_ref[0]]
    for way in range(2):
        @pl.when(can_send(0, way))
        def _():
            src_hop(0, way).start()
    def block_copy(owner, origin, target, send_sem, recv_sem):
        block = src_out.at[pl.ds(owner * part, part), pl.ds(pl.multiple_of(origin * rows, rows), rows), :]
        return pltpu.make_async_remote_copy(
            src_ref=block, dst_ref=block, send_sem=send_sem, recv_sem=recv_sem,
            device_id=(me_w, target), device_id_type=MESH)

    def chip_copy(w, d):
        return block_copy(me_r, w, lax.rem(me_r + 2 * d, n_rcv), x_send.at[w, d], x_recv.at[w, d])

    def chip_arrival(w, d):
        return block_copy(lax.rem(me_r - 2 * d + n_rcv, n_rcv), w, sibling, x_send.at[w, d], x_recv.at[w, d])

    def core_copy(w, d):
        return block_copy(lax.rem(me_r - 2 * d + n_rcv, n_rcv), w, sibling, c_send.at[w, d], c_recv.at[w, d])

    def core_arrival(w, d):
        return block_copy(lax.rem(sibling - 2 * d + n_rcv, n_rcv), w, sibling, c_send.at[w, d], c_recv.at[w, d])

    def spread_block(w):
        @pl.loop(1, n_chip)
        def _(d):
            chip_copy(w, d).start()

        core_copy(w, 0).start()

    spread_block(me_w)
    for t in range(n_win - 1):
        for way in range(2):
            @pl.when(can_receive(t, way))
            def _():
                src_arrival(t, way).wait_recv()

            @pl.when(can_send(t + 1, way))
            def _():
                src_hop(t + 1, way).start()

            @pl.when(can_receive(t, way))
            def _():
                spread_block(me_w - (1 - 2 * way) * (t + 1))

    for c in range(2, CHUNKS):
        start_own(c)

    def forward(c, t):
        for way in range(2):
            @pl.when(can_receive(t, way))
            def _():
                recv_arrival(c, t, way).wait_recv()

            @pl.when(can_send(t + 1, way))
            def _():
                recv_hop(c, t + 1, way).start()

    for t in range(n_win - 1):
        forward(0, t)

    @pl.loop(0, n_win)
    def _(w):
        @pl.loop(1, n_chip)
        def _(d):
            chip_arrival(w, d).wait_recv()
            core_copy(w, d).start()

    for t in range(n_win - 1):
        forward(1, t)

    @pl.loop(0, n_win)
    def _(w):
        @pl.loop(0, n_chip)
        def _(d):
            core_arrival(w, d).wait_recv()

    def forward_rest(t):
        for c in range(CHUNKS // HALVES, CHUNKS):
            forward(c, t)

    forward_rest(0)
    prepare_source(groups, src_out, flipped, weights)
    forward_rest(1)

    half = n_chan // HALVES
    pairs = LANES // 2
    turn_receivers(0, half, recv_out, flipped)
    cross_part(0, pairs // 2, groups, half, flipped, weights, x_real, x_imag)
    for t in range(2, n_win - 1):
        forward_rest(t)
    cross_part(pairs // 2, pairs, groups, half, flipped, weights, x_real, x_imag)
    table_local.wait()
    lags_of(0, half, lag_scale, table, x_real, x_imag, out_ref)
    turn_receivers(half, half, recv_out, flipped)
    cross_part(0, pairs, groups, half, flipped, weights, x_real, x_imag)
    lags_of(half, half, lag_scale, table, x_real, x_imag, out_ref)

    @pl.loop(0, n_win)
    def _(w):
        @pl.loop(0, n_chip)
        def _(d):
            core_copy(w, d).wait_send()

        @pl.loop(1, n_chip)
        def _(d):
            chip_copy(w, d).wait_send()

    for t in range(n_win - 1):
        for way in range(2):
            @pl.when(can_send(t, way))
            def _():
                src_hop(t, way).wait_send()
                for c in range(CHUNKS):
                    recv_hop(c, t, way).wait_send()


def fused(root, own, table, n_win, n_rcv, lag_scale, groups):
    n_chan, rows, lanes = own.shape
    part = n_chan // n_rcv
    half = n_chan // HALVES
    depth = n_win * rows
    n_lags, n_freqs = table.shape[3], table.shape[2] * lanes
    bf16 = own.dtype
    sem = pltpu.SemaphoreType.DMA
    return pl.pallas_call(
        functools.partial(fused_kernel, n_win, n_rcv, groups, lag_scale),
        out_shape=jax.ShapeDtypeStruct((n_chan, n_chan, n_lags), bf16),
        in_specs=[
            pl.BlockSpec(memory_space=pltpu.SMEM),
            pl.BlockSpec(memory_space=pl.ANY),
            pl.BlockSpec(memory_space=pl.ANY),
        ],
        out_specs=pl.BlockSpec(memory_space=pltpu.VMEM),
        scratch_shapes=[
            pltpu.VMEM((n_chan, depth, lanes), bf16),
            pltpu.VMEM((n_chan, depth, lanes), bf16),
            pltpu.VMEM((n_rcv, part, rows, lanes), bf16),
            pltpu.VMEM(table.shape[1:], bf16),
            pltpu.VMEM((depth // LANES, n_chan * lanes, LANES), jnp.float32),
            pltpu.VMEM((lanes, depth, 4 * n_chan), bf16),
            pltpu.VMEM((half // 2, n_freqs, 2 * n_chan), bf16),
            pltpu.VMEM((half // 2, n_freqs, 2 * n_chan), bf16),
            sem((n_rcv,)), sem((n_rcv,)),
            sem((2, n_win, CHUNKS)), sem((2, n_win, CHUNKS)),
            sem((2, n_win)), sem((2, n_win)),
            sem((n_win, n_rcv)), sem((n_win, n_rcv)),
            sem((n_win, n_rcv)), sem((n_win, n_rcv)),
            sem((3,)),
        ],
        compiler_params=pltpu.CompilerParams(
            collective_id=0, has_side_effects=True, vmem_limit_bytes=56 << 20),
        name="fused",
    )(root, own, table)


def body(n_win, n_rcv, spectra, source_block):
    n_chan, n_time, parts, n_freqs = spectra.shape
    groups = n_freqs // LANES
    lag_scale = 1.0 / math.sqrt(2 * n_freqs * n_time * n_win)
    table = jnp.asarray(lag_table(n_freqs, n_win, groups))
    own = spectra.reshape(n_chan, n_time * parts * groups, LANES)
    return fused(source_block, own, table, n_win, n_rcv, lag_scale, groups)


def solution(mesh):
    in_specs = (P("rcv", "win", None, None), P())
    out_specs = P("rcv", None, "win")
    fn = functools.partial(body, mesh.shape["win"], mesh.shape["rcv"])
    return jax.shard_map(fn, mesh=mesh, in_specs=in_specs, out_specs=out_specs, check_vma=False)
```

```python
import functools
import math

import jax
import jax.numpy as jnp
import ml_dtypes
import numpy as np
from jax import lax
from jax.experimental import pallas as pl
from jax.experimental.pallas import tpu as pltpu
from jax.sharding import PartitionSpec as P

MESH = pl.DeviceIdType.MESH
LANES = 128
CHUNKS = 4
HALVES = 2


def lag_table(n_freqs, n_win, groups):
    n_lags = 2 * n_freqs
    column = np.arange(n_freqs)
    freq = (column % groups) * LANES + column // groups
    lag = (np.arange(n_lags) - n_freqs).reshape(n_win, 1, n_lags // n_win, 1)
    angle = (2.0 * math.pi / n_lags) * ((freq * lag) % n_lags)
    table = np.concatenate([np.cos(angle), -np.sin(angle)], axis=1)
    slabs = table.reshape(n_win, 2, n_lags // n_win, groups, LANES).swapaxes(2, 3)
    return np.ascontiguousarray(slabs).astype(ml_dtypes.bfloat16)


def store_turned(flipped, row, block):
    turned = block.astype(jnp.float32).T
    at = pl.ds(pl.multiple_of(row * LANES, LANES), LANES)
    for slab in range(flipped.shape[0]):
        flipped[slab, at, :] = turned[:, slab * LANES:(slab + 1) * LANES]


def load_turned(flipped, j, count):
    slabs = [flipped[slab, pl.ds(j, count, stride=LANES), :] for slab in range(flipped.shape[0])]
    return jnp.concatenate(slabs, axis=1)


def prepare_source(groups, n_src, flipped, weights):
    depth = weights.shape[1]
    first_half = lax.broadcasted_iota(jnp.int32, (1, 2 * n_src), 1) < n_src

    @pl.loop(0, LANES // 2, unroll=4)
    def _(jp):
        both = jnp.concatenate([load_turned(flipped, 2 * jp, n_src), load_turned(flipped, 2 * jp + 1, n_src)], axis=0).T
        crossed = pltpu.roll(both, n_src, 1)
        for k, (low, high) in enumerate(((both, crossed), (crossed, both))):
            real = jnp.where(first_half, low, high)
            pairs = real.reshape(depth // (2 * groups), 2, groups, 2 * n_src)
            imag = jnp.stack([pairs[:, 1], -pairs[:, 0]], axis=1).reshape(depth, 2 * n_src)
            weights[2 * jp + k, :, :2 * n_src] = real.astype(jnp.bfloat16)
            weights[2 * jp + k, :, 2 * n_src:] = imag.astype(jnp.bfloat16)


def turn(first, count, row, ref, flipped):
    @pl.loop(0, count, unroll=min(count, 8))
    def _(r):
        store_turned(flipped, row + r, ref[first + r])


def cross_part(first, last, groups, n_chan, flipped, weights, x_real, x_imag):
    depth, n_src = weights.shape[1], weights.shape[2] // 4
    row = lax.broadcasted_iota(jnp.int32, (groups, LANES), 0)
    picked = lax.rem(lax.broadcasted_iota(jnp.int32, (groups, LANES), 1), groups) == row
    first_half = lax.broadcasted_iota(jnp.int32, (1, 1, 2 * n_src), 2) < n_src

    @pl.loop(first, last, unroll=4)
    def _(jp):
        reals, imags = [], []
        for k in range(2):
            j = 2 * jp + k
            slabs = []
            for slab in range(depth // LANES):
                rows = [jnp.where(picked, flipped[slab, pl.ds(r * LANES + j, 1), :], 0.0) for r in range(n_chan)]
                slabs.append(jnp.concatenate(rows, axis=0).astype(jnp.bfloat16))
            spread = jnp.concatenate(slabs, axis=1)
            cross = jnp.dot(spread, weights[j], preferred_element_type=jnp.float32)
            for half, kept in ((0, reals), (1, imags)):
                part = cross[:, half * 2 * n_src:(half + 1) * 2 * n_src].reshape(n_chan // 2, 2, groups, 2 * n_src)
                kept.append(jnp.where(first_half, part[:, 0], part[:, 1]))
        at = pl.ds(pl.multiple_of(jp * 2 * groups, 2 * groups), 2 * groups)
        x_real[:, at, :] = jnp.concatenate(reals, axis=1).astype(jnp.bfloat16)
        x_imag[:, at, :] = jnp.concatenate(imags, axis=1).astype(jnp.bfloat16)


def lags_of(first, n_chan, lag_scale, table_ref, x_real, x_imag, out_ref):
    n_src, n_lags = out_ref.shape[1:]

    @pl.loop(0, n_chan // 4, unroll=2)
    def _(q):
        real = jnp.concatenate([x_real[2 * q], x_real[2 * q + 1]], axis=1)
        imag = jnp.concatenate([x_imag[2 * q], x_imag[2 * q + 1]], axis=1)
        cosines, sines = (jnp.concatenate([table_ref[p, k] for k in range(table_ref.shape[1])], axis=1) for p in range(2))
        lagged = jnp.dot(cosines, real, preferred_element_type=jnp.float32)
        lagged += jnp.dot(sines, imag, preferred_element_type=jnp.float32)
        turned = (lagged * lag_scale).T.astype(jnp.bfloat16)
        out_ref[pl.ds(first + q * 4, 4)] = turned.reshape(4, n_src, n_lags)


def fused_kernel(n_win, n_rcv, groups, lag_scale, root_ref, own_ref, table_ref, out_ref, recv_out, src_out, slots,
                 table, result, flipped, spread_rows, weights, x_real, x_imag, sp_send, sp_recv, r_send, r_recv, z_send, z_recv, x_send, x_recv,
                 c_send, c_recv, local_sem):
    me_w = lax.axis_index("win")
    me_r = lax.axis_index("rcv")
    n_chan, rows = own_ref.shape[0], own_ref.shape[1]
    part = n_chan // n_rcv
    chunk = n_chan // CHUNKS
    sibling = me_r + 1 - 2 * lax.rem(me_r, 2)
    n_chip = n_rcv // 2

    barrier = pltpu.get_barrier_semaphore()

    @pl.when(me_w > 0)
    def _():
        pl.semaphore_signal(barrier, inc=1, device_id=(me_w - 1, me_r), device_id_type=MESH)

    @pl.when(me_w < n_win - 1)
    def _():
        pl.semaphore_signal(barrier, inc=1, device_id=(me_w + 1, me_r), device_id_type=MESH)

    @pl.loop(1, n_rcv)
    def _(d):
        pl.semaphore_signal(barrier, inc=1, device_id=(me_w, lax.rem(me_r + d, n_rcv)), device_id_type=MESH)

    on_line = (me_w > 0).astype(jnp.int32) + (me_w < n_win - 1).astype(jnp.int32)
    pl.semaphore_wait(barrier, n_rcv - 1 + on_line)

    def piece_copy(d):
        target = lax.rem(me_r + d, n_rcv)
        return pltpu.make_async_remote_copy(
            src_ref=own_ref.at[pl.ds(target * part, part)], dst_ref=slots.at[me_r],
            send_sem=sp_send.at[d], recv_sem=sp_recv.at[d],
            device_id=(me_w, target), device_id_type=MESH)

    def hop(buffer, first, count, origin, send_sem, recv_sem, step):
        block = buffer.at[pl.ds(first, count), pl.ds(origin * rows, rows), :]
        return pltpu.make_async_remote_copy(
            src_ref=block, dst_ref=block, send_sem=send_sem, recv_sem=recv_sem,
            device_id=(me_w + step, me_r), device_id_type=MESH)

    def recv_hop(c, t, way):
        step = 1 - 2 * way
        return hop(recv_out, c * chunk, chunk, me_w - step * t, r_send.at[way, t, c], r_recv.at[way, t, c], step)

    def src_hop(t, way):
        step = 1 - 2 * way
        return hop(src_out, me_r * part, part, me_w - step * t, z_send.at[way, t], z_recv.at[way, t], step)

    def can_send(t, way):
        return (me_w >= t) & (me_w < n_win - 1) if way == 0 else (me_w + t < n_win) & (me_w > 0)

    def can_receive(t, way):
        return me_w > t if way == 0 else me_w + t + 1 < n_win


    def recv_arrival(c, t, way):
        step = 1 - 2 * way
        return hop(recv_out, c * chunk, chunk, me_w - step * (t + 1), r_send.at[way, t, c], r_recv.at[way, t, c], 0)

    def src_arrival(t, way):
        step = 1 - 2 * way
        return hop(src_out, me_r * part, part, me_w - step * (t + 1), z_send.at[way, t], z_recv.at[way, t], 0)

    @pl.loop(1, n_rcv)
    def _(d):
        piece_copy(d).start()

    table_local = pltpu.make_async_copy(table_ref.at[me_w], table, local_sem.at[2])
    table_local.start()
    own_local = pltpu.make_async_copy(own_ref, recv_out.at[:, pl.ds(me_w * rows, rows), :], local_sem.at[0])
    own_local.start()
    piece_local = pltpu.make_async_copy(own_ref.at[pl.ds(me_r * part, part)], slots.at[me_r], local_sem.at[1])
    piece_local.start()
    own_local.wait()

    def start_own(c):
        for way in range(2):
            @pl.when(can_send(0, way))
            def _():
                recv_hop(c, 0, way).start()

    start_own(0)
    start_own(1)

    piece_local.wait()

    @pl.loop(1, n_rcv)
    def _(d):
        piece_copy(d).wait()

    mine = (pl.ds(me_r * part, part), pl.ds(pl.multiple_of(me_w * rows, rows), rows), slice(None))
    src_out[mine] = slots[root_ref[0]]
    for way in range(2):
        @pl.when(can_send(0, way))
        def _():
            src_hop(0, way).start()
    def block_copy(owner, origin, target, send_sem, recv_sem):
        block = src_out.at[pl.ds(owner * part, part), pl.ds(pl.multiple_of(origin * rows, rows), rows), :]
        return pltpu.make_async_remote_copy(
            src_ref=block, dst_ref=block, send_sem=send_sem, recv_sem=recv_sem,
            device_id=(me_w, target), device_id_type=MESH)

    def chip_copy(w, d):
        return block_copy(me_r, w, lax.rem(me_r + 2 * d, n_rcv), x_send.at[w, d], x_recv.at[w, d])

    def chip_arrival(w, d):
        return block_copy(lax.rem(me_r - 2 * d + n_rcv, n_rcv), w, sibling, x_send.at[w, d], x_recv.at[w, d])

    def core_copy(w, d):
        return block_copy(lax.rem(me_r - 2 * d + n_rcv, n_rcv), w, sibling, c_send.at[w, d], c_recv.at[w, d])

    def core_arrival(w, d):
        return block_copy(lax.rem(sibling - 2 * d + n_rcv, n_rcv), w, sibling, c_send.at[w, d], c_recv.at[w, d])

    def spread_block(w):
        @pl.loop(1, n_chip)
        def _(d):
            chip_copy(w, d).start()

        core_copy(w, 0).start()

    spread_block(me_w)
    for t in range(n_win - 1):
        for way in range(2):
            @pl.when(can_receive(t, way))
            def _():
                src_arrival(t, way).wait_recv()

            @pl.when(can_send(t + 1, way))
            def _():
                src_hop(t + 1, way).start()

            @pl.when(can_receive(t, way))
            def _():
                spread_block(me_w - (1 - 2 * way) * (t + 1))

    for c in range(2, CHUNKS):
        start_own(c)

    def forward(c, t):
        for way in range(2):
            @pl.when(can_receive(t, way))
            def _():
                recv_arrival(c, t, way).wait_recv()

            @pl.when(can_send(t + 1, way))
            def _():
                recv_hop(c, t + 1, way).start()

    for t in range(n_win - 1):
        forward(0, t)

    @pl.loop(0, n_win)
    def _(w):
        @pl.loop(1, n_chip)
        def _(d):
            chip_arrival(w, d).wait_recv()
            core_copy(w, d).start()

    for t in range(n_win - 1):
        forward(1, t)

    def forward_rest(t):
        for c in range(CHUNKS // HALVES, CHUNKS):
            forward(c, t)

    def turn_source(owner):
        turn(owner * part, part, owner * part, src_out, flipped)

    half = n_chan // HALVES
    turn(0, half, 0, recv_out, spread_rows)

    @pl.loop(0, n_chip)
    def _(d):
        turn_source(lax.rem(me_r - 2 * d + n_rcv, n_rcv))

    @pl.loop(0, n_win)
    def _(w):
        @pl.loop(0, n_chip)
        def _(d):
            core_arrival(w, d).wait_recv()

    forward_rest(0)

    @pl.loop(0, n_chip)
    def _(d):
        turn_source(lax.rem(sibling - 2 * d + n_rcv, n_rcv))

    prepare_source(groups, n_chan, flipped, weights)
    forward_rest(1)

    def result_copy(first, which):
        rows_of = pl.ds(first, half)
        return pltpu.make_async_copy(result.at[rows_of], out_ref.at[rows_of], local_sem.at[3 + which])

    pairs = LANES // 2
    cross_part(0, pairs // 2, groups, half, spread_rows, weights, x_real, x_imag)
    for t in range(2, n_win - 1):
        forward_rest(t)
    cross_part(pairs // 2, pairs, groups, half, spread_rows, weights, x_real, x_imag)
    table_local.wait()
    lags_of(0, half, lag_scale, table, x_real, x_imag, result)
    result_copy(0, 0).start()
    turn(half, half, 0, recv_out, spread_rows)
    cross_part(0, pairs, groups, half, spread_rows, weights, x_real, x_imag)
    lags_of(half, half, lag_scale, table, x_real, x_imag, result)
    result_copy(half, 1).start()
    result_copy(0, 0).wait()
    result_copy(half, 1).wait()

    @pl.loop(0, n_win)
    def _(w):
        @pl.loop(0, n_chip)
        def _(d):
            core_copy(w, d).wait_send()

        @pl.loop(1, n_chip)
        def _(d):
            chip_copy(w, d).wait_send()

    for t in range(n_win - 1):
        for way in range(2):
            @pl.when(can_send(t, way))
            def _():
                src_hop(t, way).wait_send()
                for c in range(CHUNKS):
                    recv_hop(c, t, way).wait_send()


def fused(root, own, table, n_win, n_rcv, lag_scale, groups):
    n_chan, rows, lanes = own.shape
    part = n_chan // n_rcv
    half = n_chan // HALVES
    depth = n_win * rows
    n_lags, n_freqs = table.shape[3], table.shape[2] * lanes
    bf16 = own.dtype
    sem = pltpu.SemaphoreType.DMA
    return pl.pallas_call(
        functools.partial(fused_kernel, n_win, n_rcv, groups, lag_scale),
        out_shape=jax.ShapeDtypeStruct((n_chan, n_chan, n_lags), bf16),
        in_specs=[
            pl.BlockSpec(memory_space=pltpu.SMEM),
            pl.BlockSpec(memory_space=pl.ANY),
            pl.BlockSpec(memory_space=pl.ANY),
        ],
        out_specs=pl.BlockSpec(memory_space=pl.ANY),
        scratch_shapes=[
            pltpu.VMEM((n_chan, depth, lanes), bf16),
            pltpu.VMEM((n_chan, depth, lanes), bf16),
            pltpu.VMEM((n_rcv, part, rows, lanes), bf16),
            pltpu.VMEM(table.shape[1:], bf16),
            pltpu.VMEM((n_chan, n_chan, n_lags), bf16),
            pltpu.VMEM((depth // LANES, n_chan * lanes, LANES), jnp.float32),
            pltpu.VMEM((depth // LANES, half * lanes, LANES), jnp.float32),
            pltpu.VMEM((lanes, depth, 4 * n_chan), bf16),
            pltpu.VMEM((half // 2, n_freqs, 2 * n_chan), bf16),
            pltpu.VMEM((half // 2, n_freqs, 2 * n_chan), bf16),
            sem((n_rcv,)), sem((n_rcv,)),
            sem((2, n_win, CHUNKS)), sem((2, n_win, CHUNKS)),
            sem((2, n_win)), sem((2, n_win)),
            sem((n_win, n_rcv)), sem((n_win, n_rcv)),
            sem((n_win, n_rcv)), sem((n_win, n_rcv)),
            sem((5,)),
        ],
        compiler_params=pltpu.CompilerParams(
            collective_id=0, has_side_effects=True, vmem_limit_bytes=58 << 20),
        name="fused",
    )(root, own, table)


def body(n_win, n_rcv, spectra, source_block):
    n_chan, n_time, parts, n_freqs = spectra.shape
    groups = n_freqs // LANES
    lag_scale = 1.0 / math.sqrt(2 * n_freqs * n_time * n_win)
    table = jnp.asarray(lag_table(n_freqs, n_win, groups))
    own = spectra.reshape(n_chan, n_time * parts * groups, LANES)
    return fused(source_block, own, table, n_win, n_rcv, lag_scale, groups)


def solution(mesh):
    in_specs = (P("rcv", "win", None, None), P())
    out_specs = P("rcv", None, "win")
    fn = functools.partial(body, mesh.shape["win"], mesh.shape["rcv"])
    return jax.shard_map(fn, mesh=mesh, in_specs=in_specs, out_specs=out_specs, check_vma=False)
```

```python
import functools
import math

import jax
import jax.numpy as jnp
import ml_dtypes
import numpy as np
from jax import lax
from jax.experimental import pallas as pl
from jax.experimental.pallas import tpu as pltpu
from jax.sharding import PartitionSpec as P

MESH = pl.DeviceIdType.MESH
LANES = 128
CHUNKS = 4
HALVES = 2


def lag_table(n_freqs, n_win, groups):
    n_lags = 2 * n_freqs
    column = np.arange(n_freqs)
    freq = (column % groups) * LANES + column // groups
    lag = (np.arange(n_lags) - n_freqs).reshape(n_win, 1, n_lags // n_win, 1)
    angle = (2.0 * math.pi / n_lags) * ((freq * lag) % n_lags)
    table = np.concatenate([np.cos(angle), -np.sin(angle)], axis=1)
    slabs = table.reshape(n_win, 2, n_lags // n_win, groups, LANES).swapaxes(2, 3)
    return np.ascontiguousarray(slabs).astype(ml_dtypes.bfloat16)


def store_turned(flipped, row, block):
    turned = block.astype(jnp.float32).T
    at = pl.ds(pl.multiple_of(row * LANES, LANES), LANES)
    for slab in range(flipped.shape[0]):
        flipped[slab, at, :] = turned[:, slab * LANES:(slab + 1) * LANES]


def load_turned(flipped, j, count):
    slabs = [flipped[slab, pl.ds(j, count, stride=LANES), :] for slab in range(flipped.shape[0])]
    return jnp.concatenate(slabs, axis=1)


def prepare_source(groups, n_src, flipped, weights):
    depth = weights.shape[1]
    first_half = lax.broadcasted_iota(jnp.int32, (1, 2 * n_src), 1) < n_src

    @pl.loop(0, LANES // 2, unroll=4)
    def _(jp):
        both = jnp.concatenate([load_turned(flipped, 2 * jp, n_src), load_turned(flipped, 2 * jp + 1, n_src)], axis=0).T
        crossed = pltpu.roll(both, n_src, 1)
        for k, (low, high) in enumerate(((both, crossed), (crossed, both))):
            real = jnp.where(first_half, low, high)
            pairs = real.reshape(depth // (2 * groups), 2, groups, 2 * n_src)
            imag = jnp.stack([pairs[:, 1], -pairs[:, 0]], axis=1).reshape(depth, 2 * n_src)
            weights[2 * jp + k, :, :2 * n_src] = real.astype(jnp.bfloat16)
            weights[2 * jp + k, :, 2 * n_src:] = imag.astype(jnp.bfloat16)


def turn(first, count, row, ref, flipped):
    @pl.loop(0, count, unroll=min(count, 8))
    def _(r):
        store_turned(flipped, row + r, ref[first + r])


def cross_part(first, last, groups, n_chan, flipped, weights, x_real, x_imag):
    depth, n_src = weights.shape[1], weights.shape[2] // 4
    row = lax.broadcasted_iota(jnp.int32, (groups, LANES), 0)
    picked = lax.rem(lax.broadcasted_iota(jnp.int32, (groups, LANES), 1), groups) == row
    first_half = lax.broadcasted_iota(jnp.int32, (1, 1, 2 * n_src), 2) < n_src

    @pl.loop(first, last, unroll=4)
    def _(jp):
        reals, imags = [], []
        for k in range(2):
            j = 2 * jp + k
            slabs = []
            for slab in range(depth // LANES):
                rows = [jnp.where(picked, flipped[slab, pl.ds(r * LANES + j, 1), :], 0.0) for r in range(n_chan)]
                slabs.append(jnp.concatenate(rows, axis=0).astype(jnp.bfloat16))
            spread = jnp.concatenate(slabs, axis=1)
            cross = jnp.dot(spread, weights[j], preferred_element_type=jnp.float32)
            for half, kept in ((0, reals), (1, imags)):
                part = cross[:, half * 2 * n_src:(half + 1) * 2 * n_src].reshape(n_chan // 2, 2, groups, 2 * n_src)
                kept.append(jnp.where(first_half, part[:, 0], part[:, 1]))
        at = pl.ds(pl.multiple_of(jp * 2 * groups, 2 * groups), 2 * groups)
        x_real[:, at, :] = jnp.concatenate(reals, axis=1).astype(jnp.bfloat16)
        x_imag[:, at, :] = jnp.concatenate(imags, axis=1).astype(jnp.bfloat16)


def lags_of(first, n_chan, lag_scale, table_ref, x_real, x_imag, out_ref):
    n_src, n_lags = out_ref.shape[1:]

    @pl.loop(0, n_chan // 4, unroll=2)
    def _(q):
        real = jnp.concatenate([x_real[2 * q], x_real[2 * q + 1]], axis=1)
        imag = jnp.concatenate([x_imag[2 * q], x_imag[2 * q + 1]], axis=1)
        cosines, sines = (jnp.concatenate([table_ref[p, k] for k in range(table_ref.shape[1])], axis=1) for p in range(2))
        lagged = jnp.dot(cosines, real, preferred_element_type=jnp.float32)
        lagged += jnp.dot(sines, imag, preferred_element_type=jnp.float32)
        turned = (lagged * lag_scale).T.astype(jnp.bfloat16)
        out_ref[pl.ds(first + q * 4, 4)] = turned.reshape(4, n_src, n_lags)


def fused_kernel(n_win, n_rcv, groups, lag_scale, root_ref, own_ref, table_ref, out_ref, recv_out, src_out, slots,
                 table, result, flipped, spread_rows, weights, x_real, x_imag, sp_send, sp_recv, r_send, r_recv, z_send, z_recv, x_send, x_recv,
                 c_send, c_recv, local_sem):
    me_w = lax.axis_index("win")
    me_r = lax.axis_index("rcv")
    n_chan, rows = own_ref.shape[0], own_ref.shape[1]
    part = n_chan // n_rcv
    chunk = n_chan // CHUNKS
    sibling = me_r + 1 - 2 * lax.rem(me_r, 2)
    n_chip = n_rcv // 2

    barrier = pltpu.get_barrier_semaphore()

    @pl.when(me_w > 0)
    def _():
        pl.semaphore_signal(barrier, inc=1, device_id=(me_w - 1, me_r), device_id_type=MESH)

    @pl.when(me_w < n_win - 1)
    def _():
        pl.semaphore_signal(barrier, inc=1, device_id=(me_w + 1, me_r), device_id_type=MESH)

    @pl.loop(1, n_rcv)
    def _(d):
        pl.semaphore_signal(barrier, inc=1, device_id=(me_w, lax.rem(me_r + d, n_rcv)), device_id_type=MESH)

    on_line = (me_w > 0).astype(jnp.int32) + (me_w < n_win - 1).astype(jnp.int32)
    pl.semaphore_wait(barrier, n_rcv - 1 + on_line)

    def piece_copy(d):
        target = lax.rem(me_r + d, n_rcv)
        return pltpu.make_async_remote_copy(
            src_ref=own_ref.at[pl.ds(target * part, part)], dst_ref=slots.at[me_r],
            send_sem=sp_send.at[d], recv_sem=sp_recv.at[d],
            device_id=(me_w, target), device_id_type=MESH)

    def hop(buffer, first, count, origin, send_sem, recv_sem, step):
        block = buffer.at[pl.ds(first, count), pl.ds(origin * rows, rows), :]
        return pltpu.make_async_remote_copy(
            src_ref=block, dst_ref=block, send_sem=send_sem, recv_sem=recv_sem,
            device_id=(me_w + step, me_r), device_id_type=MESH)

    def recv_hop(c, t, way):
        step = 1 - 2 * way
        return hop(recv_out, c * chunk, chunk, me_w - step * t, r_send.at[way, t, c], r_recv.at[way, t, c], step)

    def src_hop(t, way):
        step = 1 - 2 * way
        return hop(src_out, me_r * part, part, me_w - step * t, z_send.at[way, t], z_recv.at[way, t], step)

    def can_send(t, way):
        return (me_w >= t) & (me_w < n_win - 1) if way == 0 else (me_w + t < n_win) & (me_w > 0)

    def can_receive(t, way):
        return me_w > t if way == 0 else me_w + t + 1 < n_win


    def recv_arrival(c, t, way):
        step = 1 - 2 * way
        return hop(recv_out, c * chunk, chunk, me_w - step * (t + 1), r_send.at[way, t, c], r_recv.at[way, t, c], 0)

    def src_arrival(t, way):
        step = 1 - 2 * way
        return hop(src_out, me_r * part, part, me_w - step * (t + 1), z_send.at[way, t], z_recv.at[way, t], 0)

    @pl.loop(1, n_rcv)
    def _(d):
        piece_copy(d).start()

    table_local = pltpu.make_async_copy(table_ref.at[me_w], table, local_sem.at[2])
    table_local.start()
    own_local = pltpu.make_async_copy(own_ref, recv_out.at[:, pl.ds(me_w * rows, rows), :], local_sem.at[0])
    own_local.start()
    piece_local = pltpu.make_async_copy(own_ref.at[pl.ds(me_r * part, part)], slots.at[me_r], local_sem.at[1])
    piece_local.start()
    own_local.wait()

    def start_own(c):
        for way in range(2):
            @pl.when(can_send(0, way))
            def _():
                recv_hop(c, 0, way).start()

    start_own(0)
    start_own(1)

    piece_local.wait()

    @pl.loop(1, n_rcv)
    def _(d):
        piece_copy(d).wait()

    mine = (pl.ds(me_r * part, part), pl.ds(pl.multiple_of(me_w * rows, rows), rows), slice(None))
    src_out[mine] = slots[root_ref[0]]
    for way in range(2):
        @pl.when(can_send(0, way))
        def _():
            src_hop(0, way).start()
    def block_copy(owner, origin, target, send_sem, recv_sem):
        block = src_out.at[pl.ds(owner * part, part), pl.ds(pl.multiple_of(origin * rows, rows), rows), :]
        return pltpu.make_async_remote_copy(
            src_ref=block, dst_ref=block, send_sem=send_sem, recv_sem=recv_sem,
            device_id=(me_w, target), device_id_type=MESH)

    def chip_copy(w, d):
        return block_copy(me_r, w, lax.rem(me_r + 2 * d, n_rcv), x_send.at[w, d], x_recv.at[w, d])

    def chip_arrival(w, d):
        return block_copy(lax.rem(me_r - 2 * d + n_rcv, n_rcv), w, sibling, x_send.at[w, d], x_recv.at[w, d])

    def core_copy(w, d):
        return block_copy(lax.rem(me_r - 2 * d + n_rcv, n_rcv), w, sibling, c_send.at[w, d], c_recv.at[w, d])

    def core_arrival(w, d):
        return block_copy(lax.rem(sibling - 2 * d + n_rcv, n_rcv), w, sibling, c_send.at[w, d], c_recv.at[w, d])

    def spread_block(w):
        @pl.loop(1, n_chip)
        def _(d):
            chip_copy(w, d).start()

        core_copy(w, 0).start()

    spread_block(me_w)
    for t in range(n_win - 1):
        for way in range(2):
            @pl.when(can_receive(t, way))
            def _():
                src_arrival(t, way).wait_recv()

            @pl.when(can_send(t + 1, way))
            def _():
                src_hop(t + 1, way).start()

            @pl.when(can_receive(t, way))
            def _():
                spread_block(me_w - (1 - 2 * way) * (t + 1))

    def forward(c, t):
        for way in range(2):
            @pl.when(can_receive(t, way))
            def _():
                recv_arrival(c, t, way).wait_recv()

            @pl.when(can_send(t + 1, way))
            def _():
                recv_hop(c, t + 1, way).start()

    def forward_first(t):
        for c in range(CHUNKS // HALVES):
            forward(c, t)

    forward_first(0)

    @pl.loop(0, n_win)
    def _(w):
        @pl.loop(1, n_chip)
        def _(d):
            chip_arrival(w, d).wait_recv()
            core_copy(w, d).start()

    for t in range(1, n_win - 2):
        forward_first(t)
    for c in range(CHUNKS // HALVES, CHUNKS):
        start_own(c)

    def forward_rest(t):
        for c in range(CHUNKS // HALVES, CHUNKS):
            forward(c, t)

    def turn_source(owner):
        turn(owner * part, part, owner * part, src_out, flipped)

    half = n_chan // HALVES
    @pl.loop(0, n_chip)
    def _(d):
        turn_source(lax.rem(me_r - 2 * d + n_rcv, n_rcv))

    @pl.loop(0, n_win)
    def _(w):
        @pl.loop(0, n_chip)
        def _(d):
            core_arrival(w, d).wait_recv()

    @pl.loop(0, n_chip)
    def _(d):
        turn_source(lax.rem(sibling - 2 * d + n_rcv, n_rcv))

    prepare_source(groups, n_chan, flipped, weights)
    forward_first(n_win - 2)
    forward_rest(0)
    turn(0, half, 0, recv_out, spread_rows)

    def result_copy(first, which):
        rows_of = pl.ds(first, half)
        return pltpu.make_async_copy(result.at[rows_of], out_ref.at[rows_of], local_sem.at[3 + which])

    pairs = LANES // 2
    cross_part(0, pairs // 2, groups, half, spread_rows, weights, x_real, x_imag)
    for t in range(1, n_win - 2):
        forward_rest(t)
    cross_part(pairs // 2, pairs, groups, half, spread_rows, weights, x_real, x_imag)
    table_local.wait()
    lags_of(0, half, lag_scale, table, x_real, x_imag, result)
    result_copy(0, 0).start()
    forward_rest(n_win - 2)
    turn(half, half, 0, recv_out, spread_rows)
    cross_part(0, pairs, groups, half, spread_rows, weights, x_real, x_imag)
    lags_of(half, half, lag_scale, table, x_real, x_imag, result)
    result_copy(half, 1).start()
    result_copy(0, 0).wait()
    result_copy(half, 1).wait()

    @pl.loop(0, n_win)
    def _(w):
        @pl.loop(0, n_chip)
        def _(d):
            core_copy(w, d).wait_send()

        @pl.loop(1, n_chip)
        def _(d):
            chip_copy(w, d).wait_send()

    for t in range(n_win - 1):
        for way in range(2):
            @pl.when(can_send(t, way))
            def _():
                src_hop(t, way).wait_send()
                for c in range(CHUNKS):
                    recv_hop(c, t, way).wait_send()


def fused(root, own, table, n_win, n_rcv, lag_scale, groups):
    n_chan, rows, lanes = own.shape
    part = n_chan // n_rcv
    half = n_chan // HALVES
    depth = n_win * rows
    n_lags, n_freqs = table.shape[3], table.shape[2] * lanes
    bf16 = own.dtype
    sem = pltpu.SemaphoreType.DMA
    return pl.pallas_call(
        functools.partial(fused_kernel, n_win, n_rcv, groups, lag_scale),
        out_shape=jax.ShapeDtypeStruct((n_chan, n_chan, n_lags), bf16),
        in_specs=[
            pl.BlockSpec(memory_space=pltpu.SMEM),
            pl.BlockSpec(memory_space=pl.ANY),
            pl.BlockSpec(memory_space=pl.ANY),
        ],
        out_specs=pl.BlockSpec(memory_space=pl.ANY),
        scratch_shapes=[
            pltpu.VMEM((n_chan, depth, lanes), bf16),
            pltpu.VMEM((n_chan, depth, lanes), bf16),
            pltpu.VMEM((n_rcv, part, rows, lanes), bf16),
            pltpu.VMEM(table.shape[1:], bf16),
            pltpu.VMEM((n_chan, n_chan, n_lags), bf16),
            pltpu.VMEM((depth // LANES, n_chan * lanes, LANES), jnp.float32),
            pltpu.VMEM((depth // LANES, half * lanes, LANES), jnp.float32),
            pltpu.VMEM((lanes, depth, 4 * n_chan), bf16),
            pltpu.VMEM((half // 2, n_freqs, 2 * n_chan), bf16),
            pltpu.VMEM((half // 2, n_freqs, 2 * n_chan), bf16),
            sem((n_rcv,)), sem((n_rcv,)),
            sem((2, n_win, CHUNKS)), sem((2, n_win, CHUNKS)),
            sem((2, n_win)), sem((2, n_win)),
            sem((n_win, n_rcv)), sem((n_win, n_rcv)),
            sem((n_win, n_rcv)), sem((n_win, n_rcv)),
            sem((5,)),
        ],
        compiler_params=pltpu.CompilerParams(
            collective_id=0, has_side_effects=True, vmem_limit_bytes=58 << 20),
        name="fused",
    )(root, own, table)


def body(n_win, n_rcv, spectra, source_block):
    n_chan, n_time, parts, n_freqs = spectra.shape
    groups = n_freqs // LANES
    lag_scale = 1.0 / math.sqrt(2 * n_freqs * n_time * n_win)
    table = jnp.asarray(lag_table(n_freqs, n_win, groups))
    own = spectra.reshape(n_chan, n_time * parts * groups, LANES)
    return fused(source_block, own, table, n_win, n_rcv, lag_scale, groups)


def solution(mesh):
    in_specs = (P("rcv", "win", None, None), P())
    out_specs = P("rcv", None, "win")
    fn = functools.partial(body, mesh.shape["win"], mesh.shape["rcv"])
    return jax.shard_map(fn, mesh=mesh, in_specs=in_specs, out_specs=out_specs, check_vma=False)
```
